512 devices in a mesh: dp: 64 (over y, z), mp: 8 (over x, core).
Axes of the slice: x: 4, y: 4, z: 16, core: 2. Of those that a mesh axis runs over, the one named last changes fastest.
Arguments:
- q_gen: bfloat16 [64, 512, 4096], P('mp', 'dp'), may hold values from -300 to 300
- k_gen: bfloat16 [64, 512, 1024], P('mp', 'dp'), may hold values from -9 to 9
- v_gen: bfloat16 [64, 512, 1024], P('mp', 'dp'), may hold values from -6 to 6
- grad_gen: bfloat16 [64, 512, 4096], P('mp', 'dp'), may hold values from -6 to 6
- lengths: int32 [64], replicated, may hold values from 16 to 512, as said below
- swap_flags: int32 [2, 64], replicated, may hold values from 0 to 1, as said below
Outputs:
- attn_out: bfloat16 [64, 512, 4096], P('dp', None, 'mp')
- grad_q: bfloat16 [64, 512, 4096], P('dp', None, 'mp')
- grad_k: bfloat16 [64, 512, 1024], P('dp', None, 'mp')
- grad_v: bfloat16 [64, 512, 1024], P('dp', None, 'mp')
The draws below stay inside these ranges and needn't reach their ends.
Inputs may be any that keep to these rules, and one draw needn't show every extreme that they name: `lengths`: some rollout has exactly 512 tokens. swap_flags[r, d] == swap_flags[r, d XOR (64 / 2^(r+1))]; device 64 - 1 swaps in every round.
All inputs are finite; a program needn't handle non-finite values.
Results may differ from the reference program's by a relative error of at most 0.005.
Values may be sent and summed in bfloat16 or wider, within the bound.
A program may use at most 64 MiB of HBM per device.

```python
import math
import jax
import jax.numpy as jnp
from jax import lax

QH = 32
KVH = 8
HEAD = 128
CAP = 512
ROUNDS = 2
SEQS = 64
N_DP = 64


def shared_keys(key):
    drawn = jax.random.normal(key, (SEQS, CAP, KVH * HEAD), jnp.float32)
    return jnp.clip(drawn, -6.0, 6.0)


def draw_k_gen(key, part):
    shared = shared_keys(key)
    return shared.astype(jnp.bfloat16)


def draw_q_gen(key, part):
    key = jax.random.fold_in(key, 7)
    drawn = jax.random.normal(key, (SEQS, CAP, QH * HEAD), jnp.float32)
    return drawn.astype(jnp.bfloat16)


def draw_lengths(key, part):
    key = jax.random.fold_in(key, 11)
    lowest = max(CAP // 32, 1)
    drawn = jax.random.randint(key, (SEQS,), lowest, CAP + 1)
    longest = jax.random.randint(jax.random.fold_in(key, 1), (), 0, SEQS)
    return drawn.at[longest].set(CAP).astype(jnp.int32)


def draw_swap_flags(key, part):
    key = jax.random.fold_in(key, 13)
    coins = jax.random.randint(key, (ROUNDS, N_DP), 0, 2)
    device_ids = jnp.arange(N_DP, dtype=jnp.int32)
    rows_out = []
    for round_index in range(ROUNDS):
        partner = jnp.bitwise_xor(device_ids, N_DP >> round_index + 1)
        lower = jnp.minimum(device_ids, partner)
        picked = coins[round_index][lower]
        forced = (device_ids == N_DP - 1) | (partner == N_DP - 1)
        rows_out.append(jnp.where(forced, 1, picked))
    return jnp.stack(rows_out).astype(jnp.int32)


def steps_of(stream_key, extent, cuts, low, top_value):
    loudness = 1.0
    for dim, blocks in cuts:
        draws = jax.random.uniform(jax.random.fold_in(jax.random.fold_in(stream_key, 6), dim), (blocks,), jnp.float32, low / len(cuts), top_value / len(cuts))
        loudness = loudness * jnp.repeat(jnp.exp(draws), extent[dim] // blocks).reshape((-1,) + (1,) * (len(extent) - 1 - dim))
    return loudness


def noise(stream_key, dims, spread, reach, split=(), kind=jnp.bfloat16):
    loudness = steps_of(stream_key, dims, split, -0.22, 0.18) if split else 1.0
    result = jax.random.normal(stream_key, dims, jnp.float32) * spread * loudness
    return jnp.minimum(jnp.maximum(result, -reach), reach).astype(kind)


def setup_inputs(seed: int = 0) -> dict:
    splits = jax.random.split(jax.random.key(seed), 7)
    return {
        "q_gen": draw_q_gen(jax.random.fold_in(splits[6], 71), 0),
        "k_gen": draw_k_gen(jax.random.fold_in(splits[6], 71), 0),
        "v_gen": noise(splits[2], (SEQS, CAP, KVH * HEAD), 1.0, 6.0, ((0, 8), (1, 64))),
        "grad_gen": noise(splits[3], (SEQS, CAP, QH * HEAD), 1.0, 6.0, ((0, 8), (1, 64))),
        "lengths": draw_lengths(jax.random.fold_in(splits[6], 71), 0),
        "swap_flags": draw_swap_flags(jax.random.fold_in(splits[6], 71), 0),
    }


def one_head(q_head, k_head, v_head, grad_head, length):
    rows_seq = q_head.shape[0]
    inv_root = 1.0 / math.sqrt(q_head.shape[1])
    scores = jnp.dot(q_head, k_head.T, preferred_element_type=jnp.float32) * inv_root
    position = jnp.arange(rows_seq)
    visible = (position[None, :] <= position[:, None]) & (position[None, :] < length)
    scores = jnp.where(visible, scores, -1e+30)
    row_max = lax.optimization_barrier(jnp.max(scores, axis=-1, keepdims=True))
    weights = jnp.exp(scores - row_max)
    weights = weights / lax.optimization_barrier(jnp.sum(weights, axis=-1, keepdims=True))
    probs = weights.astype(jnp.bfloat16)
    live_rows = (position < length)[:, None]
    out_head = jnp.where(live_rows, jnp.dot(probs, v_head, preferred_element_type=jnp.float32), 0.0)
    live_grad = jnp.where(live_rows, grad_head, jnp.zeros_like(grad_head))
    dv_head = jnp.dot(probs.T, live_grad, preferred_element_type=jnp.float32)
    dprob = jnp.dot(live_grad, v_head.T, preferred_element_type=jnp.float32)
    row_delta = lax.optimization_barrier(jnp.sum(weights * dprob, axis=-1, keepdims=True))
    dscore = (weights * (dprob - row_delta) * inv_root).astype(jnp.bfloat16)
    dq_head = jnp.dot(dscore, k_head, preferred_element_type=jnp.float32)
    dk_head = jnp.dot(dscore.T, q_head, preferred_element_type=jnp.float32)
    return (out_head, dq_head, dk_head, dv_head)

def attend_sequence(queries, keys, values, grads, length, kv_heads):
    rows_seq = queries.shape[0]
    head_dim = keys.shape[1] // kv_heads
    q_heads = queries.shape[1] // head_dim
    per_group = q_heads // kv_heads
    q_split = queries.reshape(rows_seq, q_heads, head_dim).transpose(1, 0, 2)
    g_split = grads.reshape(rows_seq, q_heads, head_dim).transpose(1, 0, 2)
    k_split = jnp.repeat(keys.reshape(rows_seq, kv_heads, head_dim).transpose(1, 0, 2), per_group, axis=0)
    v_split = jnp.repeat(values.reshape(rows_seq, kv_heads, head_dim).transpose(1, 0, 2), per_group, axis=0)

    def run_head(items):
        return one_head(items[0], items[1], items[2], items[3], length)
    outs, dqs, dks, dvs = lax.map(run_head, (q_split, k_split, v_split, g_split))
    out_rows = outs.transpose(1, 0, 2).reshape(rows_seq, q_heads * head_dim).astype(jnp.bfloat16)
    dq_rows = dqs.transpose(1, 0, 2).reshape(rows_seq, q_heads * head_dim).astype(jnp.bfloat16)
    dk_rows = dks.reshape(kv_heads, per_group, rows_seq, head_dim).sum(axis=1)
    dk_rows = dk_rows.transpose(1, 0, 2).reshape(rows_seq, kv_heads * head_dim).astype(jnp.bfloat16)
    dv_rows = dvs.reshape(kv_heads, per_group, rows_seq, head_dim).sum(axis=1)
    dv_rows = dv_rows.transpose(1, 0, 2).reshape(rows_seq, kv_heads * head_dim).astype(jnp.bfloat16)
    return (out_rows, dq_rows, dk_rows, dv_rows)

def place_sequences(swap_flags, devices):
    slot_ids = jnp.arange(devices, dtype=jnp.int32)
    slot_seq = slot_ids
    for round_index in range(swap_flags.shape[0]):
        partner = jnp.bitwise_xor(slot_ids, devices >> round_index + 1)
        slot_seq = jnp.where(swap_flags[round_index] == 1, slot_seq[partner], slot_seq)
    return slot_seq

def reference(q_gen, k_gen, v_gen, grad_gen, lengths, swap_flags):

    def per_sequence(items):
        return attend_sequence(items[0], items[1], items[2], items[3], items[4], KVH)
    out_seq, dq_seq, dk_seq, dv_seq = lax.map(per_sequence, (q_gen, k_gen, v_gen, grad_gen, lengths))
    slot_seq = place_sequences(swap_flags, N_DP)
    attn_out = jnp.take(out_seq, slot_seq, axis=0)
    grad_q = jnp.take(dq_seq, slot_seq, axis=0)
    grad_k = jnp.take(dk_seq, slot_seq, axis=0)
    grad_v = jnp.take(dv_seq, slot_seq, axis=0)
    return (attn_out, grad_q, grad_k, grad_v)
```

```python
import functools
import math

import jax
import jax.numpy as jnp
from jax import lax
from jax.experimental import pallas as pl
from jax.experimental.pallas import tpu as pltpu
from jax.sharding import PartitionSpec as P

HEAD = 128
N_DP = 64
N_MP = 8
N_Z = 16
N_Y = 4
ROWS = 8
CAP = N_DP * ROWS
SEQS = 64
PER = SEQS // N_MP
GROUP = 4
TILES = 1 + GROUP
CHUNKS = ((0, 2), (2, 3), (3, 4), (4, 5))
ROW_BLOCK = 256
MESH = pl.DeviceIdType.MESH
F32 = jnp.float32
BF16 = jnp.bfloat16


def dot_nt(a, b):
    return lax.dot_general(a, b, (((1,), (1,)), ((), ())), preferred_element_type=F32)


def dot_nn(a, b):
    return lax.dot_general(a, b, (((1,), (0,)), ((), ())), preferred_element_type=F32)


def dot_tn(a, b):
    return lax.dot_general(a, b, (((0,), (0,)), ((), ())), preferred_element_type=F32)


def kernel(
    flags, lengths, q_ref, k_ref, v_ref, g_ref,
    out_ref, dq_ref, dk_ref, dv_ref,
    pack, stage, full, k_buf, v_buf, dk_acc, dv_acc,
    send_a, recv_a, send_b, recv_b, *held,
):
    dp = lax.axis_index("dp")
    mp = lax.axis_index("mp")

    barrier = pltpu.get_barrier_semaphore()

    def greet_mp(step, carry):
        peer = lax.rem(mp + step, N_MP)
        pl.semaphore_signal(barrier, inc=1, device_id=(dp, peer), device_id_type=MESH)
        return carry

    def greet_dp(step, carry):
        peer = lax.rem(dp + step, N_DP)
        pl.semaphore_signal(barrier, inc=1, device_id=(peer, mp), device_id_type=MESH)
        return carry

    lax.fori_loop(1, N_MP, greet_mp, 0)
    lax.fori_loop(1, N_DP, greet_dp, 0)

    def columns(head):
        return pl.ds(pl.multiple_of(head * HEAD, HEAD), HEAD)

    def join(upper, lower):
        both = jnp.concatenate([upper.astype(F32), lower.astype(F32)], axis=1)
        return both.astype(BF16)

    def fill(h, carry):
        pack[h, 0] = join(k_ref[:, :, columns(h)], v_ref[:, :, columns(h)])
        for j in range(GROUP):
            cols = columns(h * GROUP + j)
            pack[h, 1 + j] = join(q_ref[:, :, cols], g_ref[:, :, cols])
        return carry

    lax.fori_loop(0, N_MP, fill, 0)
    pl.semaphore_wait(barrier, N_MP - 1 + N_DP - 1)

    mine = pl.ds(pl.multiple_of(mp * PER, PER), PER)
    for c, (lo, hi) in enumerate(CHUNKS):

        def send_heads(step, carry, c=c, lo=lo, hi=hi):
            peer = lax.rem(mp + step, N_MP)
            pltpu.make_async_remote_copy(
                src_ref=pack.at[peer, lo:hi],
                dst_ref=held[c].at[:, mine],
                send_sem=send_a.at[c],
                recv_sem=recv_a.at[c],
                device_id=(dp, peer),
                device_id_type=MESH,
            ).start()
            return carry

        lax.fori_loop(1, N_MP, send_heads, 0)
        for t in range(lo, hi):
            held[c][t - lo, mine] = pack[mp, t]

    def sequence_of(slot):
        one = jnp.where(flags[1, slot] == 1, slot ^ (N_DP // 4), slot)
        return jnp.where(flags[0, one] == 1, one ^ (N_DP // 2), one)

    def wait_all(sem, ref):
        pltpu.make_async_copy(ref, ref, sem).wait()

    y, z = dp // N_Z, lax.rem(dp, N_Z)
    my_sequence = sequence_of(dp)
    for c, (lo, hi) in enumerate(CHUNKS):
        wait_all(recv_a.at[c], held[c].at[:, 0 : SEQS - PER])
        for t in range(lo, hi):
            full[t, dp] = held[c][t - lo, my_sequence]

        def send_slot(step, carry, c=c, lo=lo, hi=hi):
            turn, dy = step // N_Y, lax.rem(step, N_Y)
            half = (turn + 1) // 2
            dz = jnp.where(lax.rem(turn, 2) == 1, half, N_Z - half)
            peer = lax.rem(y + dy, N_Y) * N_Z + lax.rem(z + dz, N_Z)
            sequence = sequence_of(peer)
            for t in range(lo, hi):
                stage[t, peer] = held[c][t - lo, sequence]
            pltpu.make_async_remote_copy(
                src_ref=stage.at[lo:hi, peer],
                dst_ref=full.at[lo:hi, dp],
                send_sem=send_b.at[c],
                recv_sem=recv_b.at[c],
                device_id=(peer, mp),
                device_id_type=MESH,
            ).start()
            return carry

        lax.fori_loop(1, N_DP, send_slot, 0)

    length = lengths[my_sequence]
    scale = 1.0 / math.sqrt(HEAD)
    live = lax.broadcasted_iota(jnp.int32, (CAP, 1), 0) < length

    def halves(t):
        both = full[t].astype(F32)
        return both[:, :ROWS].reshape(CAP, HEAD), both[:, ROWS:].reshape(CAP, HEAD)

    for c, (lo, hi) in enumerate(CHUNKS):
        wait_all(recv_b.at[c], full.at[lo:hi, 0 : N_DP - 1])
        for t in range(lo, hi):
            if t == 0:
                keys, values = halves(0)
                k_buf[...] = keys.astype(BF16)
                v_buf[...] = values.astype(BF16)
                continue
            j = t - 1
            q_all, g_all = halves(t)
            q_all = q_all.astype(BF16)
            g_all = jnp.where(live, g_all, 0.0).astype(BF16)
            for first in reversed(range(0, CAP, ROW_BLOCK)):
                last = first + ROW_BLOCK
                q, g = q_all[first:last], g_all[first:last]
                k, v = k_buf[:last], v_buf[:last]
                scores = dot_nt(q, k) * scale
                row = lax.broadcasted_iota(jnp.int32, (ROW_BLOCK, last), 0) + first
                col = lax.broadcasted_iota(jnp.int32, (ROW_BLOCK, last), 1)
                scores = jnp.where(col <= row, scores, -1e30)
                top = jnp.max(scores, axis=-1, keepdims=True)
                weights = jnp.exp(scores - top)
                weights = weights / jnp.sum(weights, axis=-1, keepdims=True)
                probs = weights.astype(BF16)
                out = jnp.where(live[first:last], dot_nn(probs, v), 0.0)
                dprob = dot_nt(g, v)
                delta = jnp.sum(weights * dprob, axis=-1, keepdims=True)
                dscore = (weights * (dprob - delta) * scale).astype(BF16)
                lanes = slice(j * HEAD, (j + 1) * HEAD)
                out_ref[0, first:last, lanes] = out.astype(BF16)
                dq_ref[0, first:last, lanes] = dot_nn(dscore, k).astype(BF16)
                dv_part = dot_tn(probs, g)
                dk_part = dot_tn(dscore, q)
                if j == 0 and last == CAP:
                    dv_acc[...] = dv_part
                    dk_acc[...] = dk_part
                else:
                    dv_acc[:last] += dv_part
                    dk_acc[:last] += dk_part
    dk_ref[0] = dk_acc[...].astype(BF16)
    dv_ref[0] = dv_acc[...].astype(BF16)
    for c, (lo, hi) in enumerate(CHUNKS):
        wait_all(send_a.at[c], held[c].at[:, 0 : SEQS - PER])
        wait_all(send_b.at[c], full.at[lo:hi, 0 : N_DP - 1])


def shards(q_gen, k_gen, v_gen, grad_gen, lengths, swap_flags):
    vmem = pl.BlockSpec(memory_space=pltpu.VMEM)
    smem = pl.BlockSpec(memory_space=pltpu.SMEM)
    wide = jax.ShapeDtypeStruct((1, CAP, GROUP * HEAD), BF16)
    narrow = jax.ShapeDtypeStruct((1, CAP, HEAD), BF16)
    chunks = len(CHUNKS)
    return tuple(
        pl.pallas_call(
            kernel,
            out_shape=(wide, wide, narrow, narrow),
            in_specs=[smem, smem, vmem, vmem, vmem, vmem],
            out_specs=(vmem, vmem, vmem, vmem),
            scratch_shapes=[
                pltpu.VMEM((N_MP, TILES, PER, 2 * ROWS, HEAD), BF16),
                pltpu.VMEM((TILES, N_DP, 2 * ROWS, HEAD), BF16),
                pltpu.VMEM((TILES, N_DP, 2 * ROWS, HEAD), BF16),
                pltpu.VMEM((CAP, HEAD), BF16),
                pltpu.VMEM((CAP, HEAD), BF16),
                pltpu.VMEM((CAP, HEAD), F32),
                pltpu.VMEM((CAP, HEAD), F32),
                pltpu.SemaphoreType.DMA((chunks,)),
                pltpu.SemaphoreType.DMA((chunks,)),
                pltpu.SemaphoreType.DMA((chunks,)),
                pltpu.SemaphoreType.DMA((chunks,)),
                *(pltpu.VMEM((hi - lo, SEQS, 2 * ROWS, HEAD), BF16) for lo, hi in CHUNKS),
            ],
            compiler_params=pltpu.CompilerParams(
                collective_id=0, has_side_effects=True, vmem_limit_bytes=40 * 2**20
            ),
        )(swap_flags, lengths, q_gen, k_gen, v_gen, grad_gen)
    )


def solution(mesh):
    rollout = P("mp", "dp", None)
    trainer = P("dp", None, "mp")
    return jax.shard_map(
        shards,
        mesh=mesh,
        in_specs=(rollout, rollout, rollout, rollout, P(), P()),
        out_specs=(trainer, trainer, trainer, trainer),
        check_vma=False,
    )
```

```python
import functools
import math

import jax
import jax.numpy as jnp
from jax import lax
from jax.experimental import pallas as pl
from jax.experimental.pallas import tpu as pltpu
from jax.sharding import PartitionSpec as P

HEAD = 128
N_DP = 64
N_MP = 8
N_Z = 16
N_Y = 4
ROWS = 8
CAP = N_DP * ROWS
SEQS = 64
PER = SEQS // N_MP
GROUP = 4
TILES = 1 + GROUP
CHUNKS = ((0, 1), (1, 2), (2, 3), (3, 4), (4, 5))
ROW_BLOCK = 256
MESH = pl.DeviceIdType.MESH
F32 = jnp.float32
BF16 = jnp.bfloat16


def dot_nt(a, b):
    return lax.dot_general(a, b, (((1,), (1,)), ((), ())), preferred_element_type=F32)


def dot_nn(a, b):
    return lax.dot_general(a, b, (((1,), (0,)), ((), ())), preferred_element_type=F32)


def dot_tn(a, b):
    return lax.dot_general(a, b, (((0,), (0,)), ((), ())), preferred_element_type=F32)


def kernel(
    flags_hbm, lengths_hbm, q_hbm, k_hbm, v_hbm, g_hbm,
    out_ref, dq_ref, dk_ref, dv_ref,
    flags, lengths, q_ref, k_ref, v_ref, g_ref,
    pack, stage, full, k_buf, v_buf, dk_acc, dv_acc,
    load_sem, send_a, recv_a, send_b, recv_b, *held,
):
    dp = lax.axis_index("dp")
    mp = lax.axis_index("mp")
    y, z = dp // N_Z, lax.rem(dp, N_Z)

    loads = [
        pltpu.make_async_copy(src, dst, load_sem.at[n])
        for n, (src, dst) in enumerate(
            (
                (k_hbm, k_ref), (v_hbm, v_ref), (q_hbm, q_ref), (g_hbm, g_ref),
                (flags_hbm, flags), (lengths_hbm, lengths),
            )
        )
    ]

    def greet_mp(step, carry):
        peer = lax.rem(mp + step, N_MP)
        pl.semaphore_signal(barrier, inc=1, device_id=(dp, peer), device_id_type=MESH)
        return carry

    def greet_dp(step, carry):
        peer = lax.rem(dp + step, N_DP)
        pl.semaphore_signal(barrier, inc=1, device_id=(peer, mp), device_id_type=MESH)
        return carry

    barrier = pltpu.get_barrier_semaphore()
    for load in loads:
        load.start()
    lax.fori_loop(1, N_DP, greet_dp, 0)
    lax.fori_loop(1, N_MP, greet_mp, 0)

    def columns(head):
        return pl.ds(pl.multiple_of(head * HEAD, HEAD), HEAD)

    def join(upper, lower):
        both = jnp.concatenate([upper.astype(F32), lower.astype(F32)], axis=1)
        return both.astype(BF16)

    def fill(t):
        def fill_head(h, carry):
            if t == 0:
                pack[h, 0] = join(k_ref[:, :, columns(h)], v_ref[:, :, columns(h)])
            else:
                cols = columns(h * GROUP + t - 1)
                pack[h, t] = join(q_ref[:, :, cols], g_ref[:, :, cols])
            return carry

        lax.fori_loop(0, N_MP, fill_head, 0)

    loads[0].wait()
    loads[1].wait()
    fill(0)
    pl.semaphore_wait(barrier, N_MP - 1 + N_DP - 1)

    mine = pl.ds(pl.multiple_of(mp * PER, PER), PER)
    for c, (lo, hi) in enumerate(CHUNKS):

        def send_heads(step, carry, c=c, lo=lo, hi=hi):
            peer = lax.rem(mp + step, N_MP)
            pltpu.make_async_remote_copy(
                src_ref=pack.at[peer, lo:hi],
                dst_ref=held[c].at[:, mine],
                send_sem=send_a.at[c],
                recv_sem=recv_a.at[c],
                device_id=(dp, peer),
                device_id_type=MESH,
            ).start()
            return carry

        if c == 1:
            for load in loads[2:]:
                load.wait()
        for t in range(max(lo, 1), hi):
            fill(t)
        lax.fori_loop(1, N_MP, send_heads, 0)
        for t in range(lo, hi):
            held[c][t - lo, mine] = pack[mp, t]

    def sequence_of(slot):
        one = jnp.where(flags[1, slot] == 1, slot ^ (N_DP // 4), slot)
        return jnp.where(flags[0, one] == 1, one ^ (N_DP // 2), one)

    def wait_all(sem, ref):
        pltpu.make_async_copy(ref, ref, sem).wait()

    my_sequence = sequence_of(dp)
    for c, (lo, hi) in enumerate(CHUNKS):
        wait_all(recv_a.at[c], held[c].at[:, 0 : SEQS - PER])
        for t in range(lo, hi):
            full[t, dp] = held[c][t - lo, my_sequence]

        def send_slot(step, carry, c=c, lo=lo, hi=hi):
            turn, dy = step // N_Y, lax.rem(step, N_Y)
            j = (turn - 1) // 2
            wrapped = jnp.maximum(z - 7, 0)
            up = jnp.where(j < wrapped, j, jnp.where(wrapped == 0, z + 1 + j, N_Z - 1 - (j - wrapped)))
            low = jnp.minimum(z, 7)
            down = jnp.where(j < low, wrapped + j, N_Z - 1 - (j - low))
            to_z = jnp.where(turn == 0, z, jnp.where(lax.rem(turn, 2) == 1, up, down))
            peer = lax.rem(y + dy, N_Y) * N_Z + to_z
            sequence = sequence_of(peer)
            for t in range(lo, hi):
                stage[t, peer] = held[c][t - lo, sequence]
            pltpu.make_async_remote_copy(
                src_ref=stage.at[lo:hi, peer],
                dst_ref=full.at[lo:hi, dp],
                send_sem=send_b.at[c],
                recv_sem=recv_b.at[c],
                device_id=(peer, mp),
                device_id_type=MESH,
            ).start()
            return carry

        lax.fori_loop(1, N_DP, send_slot, 0)

    length = lengths[my_sequence]
    scale = 1.0 / math.sqrt(HEAD)
    live = lax.broadcasted_iota(jnp.int32, (CAP, 1), 0) < length

    def halves(t):
        both = full[t].astype(F32)
        return both[:, :ROWS].reshape(CAP, HEAD), both[:, ROWS:].reshape(CAP, HEAD)

    for c, (lo, hi) in enumerate(CHUNKS):
        wait_all(recv_b.at[c], full.at[lo:hi, 0 : N_DP - 1])
        for t in range(lo, hi):
            if t == 0:
                keys, values = halves(0)
                k_buf[...] = keys.astype(BF16)
                v_buf[...] = values.astype(BF16)
                continue
            j = t - 1
            q_all, g_all = halves(t)
            q_all = q_all.astype(BF16)
            g_all = jnp.where(live, g_all, 0.0).astype(BF16)
            for first in reversed(range(0, CAP, ROW_BLOCK)):
                last = first + ROW_BLOCK
                q, g = q_all[first:last], g_all[first:last]
                k, v = k_buf[:last], v_buf[:last]
                scores = dot_nt(q, k) * scale
                row = lax.broadcasted_iota(jnp.int32, (ROW_BLOCK, last), 0) + first
                col = lax.broadcasted_iota(jnp.int32, (ROW_BLOCK, last), 1)
                scores = jnp.where(col <= row, scores, -1e30)
                top = jnp.max(scores, axis=-1, keepdims=True)
                weights = jnp.exp(scores - top)
                weights = weights / jnp.sum(weights, axis=-1, keepdims=True)
                probs = weights.astype(BF16)
                out = jnp.where(live[first:last], dot_nn(probs, v), 0.0)
                dprob = dot_nt(g, v)
                delta = jnp.sum(weights * dprob, axis=-1, keepdims=True)
                dscore = (weights * (dprob - delta) * scale).astype(BF16)
                lanes = slice(j * HEAD, (j + 1) * HEAD)
                out_ref[0, first:last, lanes] = out.astype(BF16)
                dq_ref[0, first:last, lanes] = dot_nn(dscore, k).astype(BF16)
                dv_part = dot_tn(probs, g)
                dk_part = dot_tn(dscore, q)
                if j == 0 and last == CAP:
                    dv_acc[...] = dv_part
                    dk_acc[...] = dk_part
                else:
                    dv_acc[:last] += dv_part
                    dk_acc[:last] += dk_part
    dk_ref[0] = dk_acc[...].astype(BF16)
    dv_ref[0] = dv_acc[...].astype(BF16)
    for c, (lo, hi) in enumerate(CHUNKS):
        wait_all(send_a.at[c], held[c].at[:, 0 : SEQS - PER])
        wait_all(send_b.at[c], full.at[lo:hi, 0 : N_DP - 1])


def write_out(*refs):
    sources, results, held, sem_in, sem_out = refs[:4], refs[4:8], refs[8:12], *refs[12:]
    loads = [pltpu.make_async_copy(*pair, sem_in.at[n]) for n, pair in enumerate(zip(sources, held))]
    stores = [pltpu.make_async_copy(*pair, sem_out.at[n]) for n, pair in enumerate(zip(held, results))]
    for load in loads:
        load.start()
    for load, store in zip(loads, stores):
        load.wait()
        store.start()
    for store in stores:
        store.wait()


def shards(q_gen, k_gen, v_gen, grad_gen, lengths, swap_flags):
    vmem = pl.BlockSpec(memory_space=pltpu.VMEM)
    hbm = pl.BlockSpec(memory_space=pl.ANY)
    wide = jax.ShapeDtypeStruct((1, CAP, GROUP * HEAD), BF16)
    narrow = jax.ShapeDtypeStruct((1, CAP, HEAD), BF16)
    chunks = len(CHUNKS)
    results = pl.pallas_call(
        kernel,
        out_shape=(wide, wide, narrow, narrow),
        in_specs=[hbm] * 6,
        out_specs=(vmem, vmem, vmem, vmem),
        scratch_shapes=[
            pltpu.SMEM(swap_flags.shape, jnp.int32),
            pltpu.SMEM(lengths.shape, jnp.int32),
            pltpu.VMEM(q_gen.shape, BF16),
            pltpu.VMEM(k_gen.shape, BF16),
            pltpu.VMEM(v_gen.shape, BF16),
            pltpu.VMEM(grad_gen.shape, BF16),
            pltpu.VMEM((N_MP, TILES, PER, 2 * ROWS, HEAD), BF16),
            pltpu.VMEM((TILES, N_DP, 2 * ROWS, HEAD), BF16),
            pltpu.VMEM((TILES, N_DP, 2 * ROWS, HEAD), BF16),
            pltpu.VMEM((CAP, HEAD), BF16),
            pltpu.VMEM((CAP, HEAD), BF16),
            pltpu.VMEM((CAP, HEAD), F32),
            pltpu.VMEM((CAP, HEAD), F32),
            pltpu.SemaphoreType.DMA((6,)),
            pltpu.SemaphoreType.DMA((chunks,)),
            pltpu.SemaphoreType.DMA((chunks,)),
            pltpu.SemaphoreType.DMA((chunks,)),
            pltpu.SemaphoreType.DMA((chunks,)),
            *(pltpu.VMEM((hi - lo, SEQS, 2 * ROWS, HEAD), BF16) for lo, hi in CHUNKS),
        ],
        compiler_params=pltpu.CompilerParams(
            collective_id=0, has_side_effects=True, vmem_limit_bytes=56 * 2**20
        ),
    )(swap_flags, lengths, q_gen, k_gen, v_gen, grad_gen)
    return tuple(
        pl.pallas_call(
            write_out,
            out_shape=(wide, wide, narrow, narrow),
            in_specs=[hbm] * 4,
            out_specs=(hbm, hbm, hbm, hbm),
            scratch_shapes=[
                *(pltpu.VMEM(result.shape, BF16) for result in (wide, wide, narrow, narrow)),
                pltpu.SemaphoreType.DMA((4,)),
                pltpu.SemaphoreType.DMA((4,)),
            ],
            compiler_params=pltpu.CompilerParams(vmem_limit_bytes=56 * 2**20),
        )(*results)
    )


def solution(mesh):
    rollout = P("mp", "dp", None)
    trainer = P("dp", None, "mp")
    return jax.shard_map(
        shards,
        mesh=mesh,
        in_specs=(rollout, rollout, rollout, rollout, P(), P()),
        out_specs=(trainer, trainer, trainer, trainer),
        check_vma=False,
    )
```

```python
import functools
import math

import jax
import jax.numpy as jnp
from jax import lax
from jax.experimental import pallas as pl
from jax.experimental.pallas import tpu as pltpu
from jax.sharding import PartitionSpec as P

HEAD = 128
N_DP = 64
N_MP = 8
N_Z = 16
N_Y = 4
ROWS = 8
CAP = N_DP * ROWS
SEQS = 64
PER = SEQS // N_MP
GROUP = 4
TILES = 1 + GROUP
CHUNKS = ((1, 2), (2, 3), (3, 4), (4, 5))
ROW_BLOCK = 256
MESH = pl.DeviceIdType.MESH
F32 = jnp.float32
BF16 = jnp.bfloat16


def dot_nt(a, b):
    return lax.dot_general(a, b, (((1,), (1,)), ((), ())), preferred_element_type=F32)


def dot_nn(a, b):
    return lax.dot_general(a, b, (((1,), (0,)), ((), ())), preferred_element_type=F32)


def dot_tn(a, b):
    return lax.dot_general(a, b, (((0,), (0,)), ((), ())), preferred_element_type=F32)


def kernel(
    flags_hbm, lengths_hbm, q_hbm, k_hbm, v_hbm, g_hbm,
    out_ref, dq_ref, dk_ref, dv_ref,
    flags, lengths, q_ref, k_ref, v_ref, g_ref,
    pack, pack_kv, by_z, by_x, by_y, stage, full, k_buf, v_buf, dk_acc, dv_acc,
    load_sem, send_kv, recv_kv, send_a, recv_a, send_b, recv_b, *held,
):
    dp = lax.axis_index("dp")
    mp = lax.axis_index("mp")
    y, z = dp // N_Z, lax.rem(dp, N_Z)
    x, core = mp // 2, lax.rem(mp, 2)
    hub = core == z // PER

    loads = [
        pltpu.make_async_copy(src, dst, load_sem.at[n])
        for n, (src, dst) in enumerate(
            (
                (k_hbm, k_ref), (v_hbm, v_ref), (q_hbm, q_ref), (g_hbm, g_ref),
                (flags_hbm, flags), (lengths_hbm, lengths),
            )
        )
    ]

    def greet_mp(step, carry):
        peer = lax.rem(mp + step, N_MP)
        pl.semaphore_signal(barrier, inc=1, device_id=(dp, peer), device_id_type=MESH)
        return carry

    def greet_dp(step, carry):
        peer = lax.rem(dp + step, N_DP)
        pl.semaphore_signal(barrier, inc=1, device_id=(peer, mp), device_id_type=MESH)
        return carry

    barrier = pltpu.get_barrier_semaphore()
    for load in loads:
        load.start()
    lax.fori_loop(1, N_DP, greet_dp, 0)
    lax.fori_loop(1, N_MP, greet_mp, 0)

    def columns(head):
        return pl.ds(pl.multiple_of(head * HEAD, HEAD), HEAD)

    def join(upper, lower):
        both = jnp.concatenate([upper.astype(F32), lower.astype(F32)], axis=1)
        return both.astype(BF16)

    def fill(t):
        def fill_head(h, carry):
            cols = columns(h * GROUP + t - 1)
            pack[h, t - 1] = join(q_ref[:, :, cols], g_ref[:, :, cols])
            return carry

        lax.fori_loop(0, N_MP, fill_head, 0)

    def fill_kv(h, carry):
        pack_kv[:, h] = join(k_ref[:, :, columns(h)], v_ref[:, :, columns(h)])
        return carry

    def remote(src, dst, send, recv, device):
        pltpu.make_async_remote_copy(
            src_ref=src, dst_ref=dst, send_sem=send, recv_sem=recv, device_id=device, device_id_type=MESH
        ).start()

    def wait_all(sem, ref):
        pltpu.make_async_copy(ref, ref, sem).wait()

    loads[0].wait()
    loads[1].wait()
    lax.fori_loop(0, N_MP, fill_kv, 0)
    pl.semaphore_wait(barrier, N_MP - 1 + N_DP - 1)

    own = lax.rem(z, PER)

    def send_kv_z(step, carry):
        i = lax.rem(own + step, PER)
        remote(pack_kv.at[i], by_z.at[z], send_kv.at[0], recv_kv.at[0], (y * N_Z + core * PER + i, mp))
        return carry

    lax.fori_loop(1, PER, send_kv_z, 0)

    @pl.when(hub)
    def _():
        by_z[z] = pack_kv[own]

    @pl.when(jnp.logical_not(hub))
    def _():
        send_kv_z(0, 0)

    mine = pl.ds(pl.multiple_of(mp * PER, PER), PER)
    for c, (lo, hi) in enumerate(CHUNKS):

        def send_heads(step, carry, c=c, lo=lo, hi=hi):
            peer = lax.rem(mp + step, N_MP)
            pltpu.make_async_remote_copy(
                src_ref=pack.at[peer, lo - 1 : hi - 1],
                dst_ref=held[c].at[:, mine],
                send_sem=send_a.at[c],
                recv_sem=recv_a.at[c],
                device_id=(dp, peer),
                device_id_type=MESH,
            ).start()
            return carry

        if c == 0:
            for load in loads[2:]:
                load.wait()
        for t in range(lo, hi):
            fill(t)
        lax.fori_loop(1, N_MP, send_heads, 0)
        for t in range(lo, hi):
            held[c][t - lo, mine] = pack[mp, t - 1]

    def sequence_of(slot):
        one = jnp.where(flags[1, slot] == 1, slot ^ (N_DP // 4), slot)
        return jnp.where(flags[0, one] == 1, one ^ (N_DP // 2), one)

    def send_kv_x():
        @pl.when(hub)
        def _():
            wait_all(recv_kv.at[0], by_z.at[0 : N_Z - 1])

            def send(step, carry):
                peer = lax.rem(mp + step, N_MP)
                remote(by_z.at[:, peer], by_x.at[x], send_kv.at[1], recv_kv.at[1], (dp, peer))
                return carry

            lax.fori_loop(1, N_MP, send, 0)
            by_x[x] = by_z[:, mp]

    def send_kv_y():
        @pl.when(hub)
        def _():
            wait_all(recv_kv.at[1], by_x.at[0 : N_Y - 1])

        @pl.when(jnp.logical_not(hub))
        def _():
            wait_all(recv_kv.at[1], by_x)

        def send(step, carry):
            to_y = lax.rem(y + step, N_Y)
            slot = to_y * N_Z + z
            by_y[to_y] = by_x[sequence_of(slot) // N_Z]
            remote(by_y.at[to_y], full.at[0, from_here], send_kv.at[2], recv_kv.at[2], (slot, mp))
            return carry

        from_here = pl.ds(pl.multiple_of(y * N_Z, N_Z), N_Z)
        lax.fori_loop(1, N_Y, send, 0)
        full[0, from_here] = by_x[my_sequence // N_Z]

    my_sequence = sequence_of(dp)
    for c, (lo, hi) in enumerate(CHUNKS):
        wait_all(recv_a.at[c], held[c].at[:, 0 : SEQS - PER])
        for t in range(lo, hi):
            full[t, dp] = held[c][t - lo, my_sequence]

        def send_slot(step, carry, c=c, lo=lo, hi=hi):
            turn, dy = step // N_Y, lax.rem(step, N_Y)
            j = (turn - 1) // 2
            wrapped = jnp.maximum(z - 7, 0)
            up = jnp.where(j < wrapped, j, jnp.where(wrapped == 0, z + 1 + j, N_Z - 1 - (j - wrapped)))
            low = jnp.minimum(z, 7)
            down = jnp.where(j < low, wrapped + j, N_Z - 1 - (j - low))
            to_z = jnp.where(turn == 0, z, jnp.where(lax.rem(turn, 2) == 1, up, down))
            peer = lax.rem(y + dy, N_Y) * N_Z + to_z
            sequence = sequence_of(peer)
            for t in range(lo, hi):
                stage[t - 1, peer] = held[c][t - lo, sequence]
            pltpu.make_async_remote_copy(
                src_ref=stage.at[lo - 1 : hi - 1, peer],
                dst_ref=full.at[lo:hi, dp],
                send_sem=send_b.at[c],
                recv_sem=recv_b.at[c],
                device_id=(peer, mp),
                device_id_type=MESH,
            ).start()
            return carry

        lax.fori_loop(1, N_DP, send_slot, 0)
        if c == 0:
            send_kv_x()
        if c == 1:
            send_kv_y()

    length = lengths[my_sequence]
    scale = 1.0 / math.sqrt(HEAD)
    live = lax.broadcasted_iota(jnp.int32, (CAP, 1), 0) < length

    def halves(t):
        both = full[t].astype(F32)
        return both[:, :ROWS].reshape(CAP, HEAD), both[:, ROWS:].reshape(CAP, HEAD)

    wait_all(recv_kv.at[2], full.at[0, 0 : N_DP - N_Z])
    keys, values = halves(0)
    k_buf[...] = keys.astype(BF16)
    v_buf[...] = values.astype(BF16)
    for c, (lo, hi) in enumerate(CHUNKS):
        wait_all(recv_b.at[c], full.at[lo:hi, 0 : N_DP - 1])
        for t in range(lo, hi):
            j = t - 1
            q_all, g_all = halves(t)
            q_all = q_all.astype(BF16)
            g_all = jnp.where(live, g_all, 0.0).astype(BF16)
            for first in reversed(range(0, CAP, ROW_BLOCK)):
                last = first + ROW_BLOCK
                q, g = q_all[first:last], g_all[first:last]
                k, v = k_buf[:last], v_buf[:last]
                scores = dot_nt(q, k) * scale
                row = lax.broadcasted_iota(jnp.int32, (ROW_BLOCK, last), 0) + first
                col = lax.broadcasted_iota(jnp.int32, (ROW_BLOCK, last), 1)
                scores = jnp.where(col <= row, scores, -1e30)
                top = jnp.max(scores, axis=-1, keepdims=True)
                weights = jnp.exp(scores - top)
                weights = weights / jnp.sum(weights, axis=-1, keepdims=True)
                probs = weights.astype(BF16)
                out = jnp.where(live[first:last], dot_nn(probs, v), 0.0)
                dprob = dot_nt(g, v)
                delta = jnp.sum(weights * dprob, axis=-1, keepdims=True)
                dscore = (weights * (dprob - delta) * scale).astype(BF16)
                lanes = slice(j * HEAD, (j + 1) * HEAD)
                out_ref[0, first:last, lanes] = out.astype(BF16)
                dq_ref[0, first:last, lanes] = dot_nn(dscore, k).astype(BF16)
                dv_part = dot_tn(probs, g)
                dk_part = dot_tn(dscore, q)
                if j == 0 and last == CAP:
                    dv_acc[...] = dv_part
                    dk_acc[...] = dk_part
                else:
                    dv_acc[:last] += dv_part
                    dk_acc[:last] += dk_part
    dk_ref[0] = dk_acc[...].astype(BF16)
    dv_ref[0] = dv_acc[...].astype(BF16)
    @pl.when(hub)
    def _():
        wait_all(send_kv.at[0], pack_kv.at[0 : PER - 1])
        wait_all(send_kv.at[1], by_z.at[:, 0 : N_MP - 1])

    @pl.when(jnp.logical_not(hub))
    def _():
        wait_all(send_kv.at[0], pack_kv)

    wait_all(send_kv.at[2], full.at[0, 0 : N_DP - N_Z])
    for c, (lo, hi) in enumerate(CHUNKS):
        wait_all(send_a.at[c], held[c].at[:, 0 : SEQS - PER])
        wait_all(send_b.at[c], full.at[lo:hi, 0 : N_DP - 1])


def write_out(*refs):
    sources, results, held, sem_in, sem_out = refs[:4], refs[4:8], refs[8:12], *refs[12:]
    loads = [pltpu.make_async_copy(*pair, sem_in.at[n]) for n, pair in enumerate(zip(sources, held))]
    stores = [pltpu.make_async_copy(*pair, sem_out.at[n]) for n, pair in enumerate(zip(held, results))]
    for load in loads:
        load.start()
    for load, store in zip(loads, stores):
        load.wait()
        store.start()
    for store in stores:
        store.wait()


def shards(q_gen, k_gen, v_gen, grad_gen, lengths, swap_flags):
    vmem = pl.BlockSpec(memory_space=pltpu.VMEM)
    hbm = pl.BlockSpec(memory_space=pl.ANY)
    wide = jax.ShapeDtypeStruct((1, CAP, GROUP * HEAD), BF16)
    narrow = jax.ShapeDtypeStruct((1, CAP, HEAD), BF16)
    chunks = len(CHUNKS)
    results = pl.pallas_call(
        kernel,
        out_shape=(wide, wide, narrow, narrow),
        in_specs=[hbm] * 6,
        out_specs=(vmem, vmem, vmem, vmem),
        scratch_shapes=[
            pltpu.SMEM(swap_flags.shape, jnp.int32),
            pltpu.SMEM(lengths.shape, jnp.int32),
            pltpu.VMEM(q_gen.shape, BF16),
            pltpu.VMEM(k_gen.shape, BF16),
            pltpu.VMEM(v_gen.shape, BF16),
            pltpu.VMEM(grad_gen.shape, BF16),
            pltpu.VMEM((N_MP, GROUP, PER, 2 * ROWS, HEAD), BF16),
            pltpu.VMEM((PER, N_MP, 2 * ROWS, HEAD), BF16),
            pltpu.VMEM((N_Z, N_MP, 2 * ROWS, HEAD), BF16),
            pltpu.VMEM((N_Y, N_Z, 2 * ROWS, HEAD), BF16),
            pltpu.VMEM((N_Y, N_Z, 2 * ROWS, HEAD), BF16),
            pltpu.VMEM((GROUP, N_DP, 2 * ROWS, HEAD), BF16),
            pltpu.VMEM((TILES, N_DP, 2 * ROWS, HEAD), BF16),
            pltpu.VMEM((CAP, HEAD), BF16),
            pltpu.VMEM((CAP, HEAD), BF16),
            pltpu.VMEM((CAP, HEAD), F32),
            pltpu.VMEM((CAP, HEAD), F32),
            pltpu.SemaphoreType.DMA((6,)),
            pltpu.SemaphoreType.DMA((3,)),
            pltpu.SemaphoreType.DMA((3,)),
            pltpu.SemaphoreType.DMA((chunks,)),
            pltpu.SemaphoreType.DMA((chunks,)),
            pltpu.SemaphoreType.DMA((chunks,)),
            pltpu.SemaphoreType.DMA((chunks,)),
            *(pltpu.VMEM((hi - lo, SEQS, 2 * ROWS, HEAD), BF16) for lo, hi in CHUNKS),
        ],
        compiler_params=pltpu.CompilerParams(
            collective_id=0, has_side_effects=True, vmem_limit_bytes=56 * 2**20
        ),
    )(swap_flags, lengths, q_gen, k_gen, v_gen, grad_gen)
    return tuple(
        pl.pallas_call(
            write_out,
            out_shape=(wide, wide, narrow, narrow),
            in_specs=[hbm] * 4,
            out_specs=(hbm, hbm, hbm, hbm),
            scratch_shapes=[
                *(pltpu.VMEM(result.shape, BF16) for result in (wide, wide, narrow, narrow)),
                pltpu.SemaphoreType.DMA((4,)),
                pltpu.SemaphoreType.DMA((4,)),
            ],
            compiler_params=pltpu.CompilerParams(vmem_limit_bytes=56 * 2**20),
        )(*results)
    )


def solution(mesh):
    rollout = P("mp", "dp", None)
    trainer = P("dp", None, "mp")
    return jax.shard_map(
        shards,
        mesh=mesh,
        in_specs=(rollout, rollout, rollout, rollout, P(), P()),
        out_specs=(trainer, trainer, trainer, trainer),
        check_vma=False,
    )
```

```python
import functools
import math

import jax
import jax.numpy as jnp
from jax import lax
from jax.experimental import pallas as pl
from jax.experimental.pallas import tpu as pltpu
from jax.sharding import PartitionSpec as P

HEAD = 128
N_DP = 64
N_MP = 8
N_Z = 16
N_Y = 4
ROWS = 8
CAP = N_DP * ROWS
SEQS = 64
PER = SEQS // N_MP
GROUP = 4
TILES = 1 + GROUP
CHUNKS = ((1, 2), (2, 3), (3, 4), (4, 5))
ROW_BLOCK = 512
MESH = pl.DeviceIdType.MESH
F32 = jnp.float32
BF16 = jnp.bfloat16


def dot_nt(a, b):
    return lax.dot_general(a, b, (((1,), (1,)), ((), ())), preferred_element_type=F32)


def dot_nn(a, b):
    return lax.dot_general(a, b, (((1,), (0,)), ((), ())), preferred_element_type=F32)


def dot_tn(a, b):
    return lax.dot_general(a, b, (((0,), (0,)), ((), ())), preferred_element_type=F32)


def kernel(
    flags_hbm, lengths_hbm, q_hbm, k_hbm, v_hbm, g_hbm,
    out_ref, dq_ref, dk_ref, dv_ref,
    flags, lengths, q_ref, k_ref, v_ref, g_ref,
    pack, pack_kv, by_z, by_x, by_y, stage, full, k_buf, v_buf, dk_acc, dv_acc,
    load_sem, send_kv, recv_kv, send_a, recv_a, send_b, recv_b, *held,
):
    dp = lax.axis_index("dp")
    mp = lax.axis_index("mp")
    y, z = dp // N_Z, lax.rem(dp, N_Z)
    x, core = mp // 2, lax.rem(mp, 2)
    hub = core == z // PER

    loads = [
        pltpu.make_async_copy(src, dst, load_sem.at[n])
        for n, (src, dst) in enumerate(
            (
                (k_hbm, k_ref), (v_hbm, v_ref), (q_hbm, q_ref), (g_hbm, g_ref),
                (flags_hbm, flags), (lengths_hbm, lengths),
            )
        )
    ]

    def greet_mp(step, carry):
        peer = lax.rem(mp + step, N_MP)
        pl.semaphore_signal(barrier, inc=1, device_id=(dp, peer), device_id_type=MESH)
        return carry

    def greet_dp(step, carry):
        peer = lax.rem(dp + step, N_DP)
        pl.semaphore_signal(barrier, inc=1, device_id=(peer, mp), device_id_type=MESH)
        return carry

    barrier = pltpu.get_barrier_semaphore()
    for load in loads:
        load.start()
    lax.fori_loop(1, N_DP, greet_dp, 0)
    lax.fori_loop(1, N_MP, greet_mp, 0)

    def columns(head):
        return pl.ds(pl.multiple_of(head * HEAD, HEAD), HEAD)

    def join(upper, lower):
        both = jnp.concatenate([upper.astype(F32), lower.astype(F32)], axis=1)
        return both.astype(BF16)

    def fill(t):
        def fill_head(h, carry):
            cols = columns(h * GROUP + t - 1)
            pack[h, t - 1] = join(q_ref[:, :, cols], g_ref[:, :, cols])
            return carry

        lax.fori_loop(0, N_MP, fill_head, 0)

    def fill_kv(h, carry):
        pack_kv[:, h] = join(k_ref[:, :, columns(h)], v_ref[:, :, columns(h)])
        return carry

    def remote(src, dst, send, recv, device):
        pltpu.make_async_remote_copy(
            src_ref=src, dst_ref=dst, send_sem=send, recv_sem=recv, device_id=device, device_id_type=MESH
        ).start()

    def wait_all(sem, ref):
        pltpu.make_async_copy(ref, ref, sem).wait()

    loads[0].wait()
    loads[1].wait()
    lax.fori_loop(0, N_MP, fill_kv, 0)
    pl.semaphore_wait(barrier, N_MP - 1 + N_DP - 1)

    own = lax.rem(z, PER)

    def send_kv_z(step, carry):
        i = lax.rem(own + step, PER)
        remote(pack_kv.at[i], by_z.at[z], send_kv.at[0], recv_kv.at[0], (y * N_Z + core * PER + i, mp))
        return carry

    lax.fori_loop(1, PER, send_kv_z, 0)

    @pl.when(hub)
    def _():
        by_z[z] = pack_kv[own]

    @pl.when(jnp.logical_not(hub))
    def _():
        send_kv_z(0, 0)

    mine = pl.ds(pl.multiple_of(mp * PER, PER), PER)
    for c, (lo, hi) in enumerate(CHUNKS):

        def send_heads(step, carry, c=c, lo=lo, hi=hi):
            peer = lax.rem(mp + step, N_MP)
            pltpu.make_async_remote_copy(
                src_ref=pack.at[peer, lo - 1 : hi - 1],
                dst_ref=held[c].at[:, mine],
                send_sem=send_a.at[c],
                recv_sem=recv_a.at[c],
                device_id=(dp, peer),
                device_id_type=MESH,
            ).start()
            return carry

        if c == 0:
            for load in loads[2:]:
                load.wait()
        for t in range(lo, hi):
            fill(t)
        lax.fori_loop(1, N_MP, send_heads, 0)
        for t in range(lo, hi):
            held[c][t - lo, mine] = pack[mp, t - 1]

    def sequence_of(slot):
        one = jnp.where(flags[1, slot] == 1, slot ^ (N_DP // 4), slot)
        return jnp.where(flags[0, one] == 1, one ^ (N_DP // 2), one)

    def send_kv_x():
        @pl.when(hub)
        def _():
            wait_all(recv_kv.at[0], by_z.at[0 : N_Z - 1])

            def send(step, carry):
                peer = lax.rem(mp + step, N_MP)
                remote(by_z.at[:, peer], by_x.at[x], send_kv.at[1], recv_kv.at[1], (dp, peer))
                return carry

            lax.fori_loop(1, N_MP, send, 0)
            by_x[x] = by_z[:, mp]

    def send_kv_y():
        @pl.when(hub)
        def _():
            wait_all(recv_kv.at[1], by_x.at[0 : N_Y - 1])

        @pl.when(jnp.logical_not(hub))
        def _():
            wait_all(recv_kv.at[1], by_x)

        def send(step, carry):
            to_y = lax.rem(y + step, N_Y)
            slot = to_y * N_Z + z
            by_y[to_y] = by_x[sequence_of(slot) // N_Z]
            remote(by_y.at[to_y], full.at[0, from_here], send_kv.at[2], recv_kv.at[2], (slot, mp))
            return carry

        from_here = pl.ds(pl.multiple_of(y * N_Z, N_Z), N_Z)
        lax.fori_loop(1, N_Y, send, 0)
        full[0, from_here] = by_x[my_sequence // N_Z]

    my_sequence = sequence_of(dp)
    for c, (lo, hi) in enumerate(CHUNKS):
        wait_all(recv_a.at[c], held[c].at[:, 0 : SEQS - PER])
        for t in range(lo, hi):
            full[t, dp] = held[c][t - lo, my_sequence]

        def send_slot(step, carry, c=c, lo=lo, hi=hi):
            turn, dy = step // N_Y, lax.rem(step, N_Y)
            j = (turn - 1) // 2
            wrapped = jnp.maximum(z - 7, 0)
            up = jnp.where(j < wrapped, j, jnp.where(wrapped == 0, z + 1 + j, N_Z - 1 - (j - wrapped)))
            low = jnp.minimum(z, 7)
            down = jnp.where(j < low, wrapped + j, N_Z - 1 - (j - low))
            to_z = jnp.where(turn == 0, z, jnp.where(lax.rem(turn, 2) == 1, up, down))
            peer = lax.rem(y + dy, N_Y) * N_Z + to_z
            sequence = sequence_of(peer)
            for t in range(lo, hi):
                stage[t - 1, peer] = held[c][t - lo, sequence]
            pltpu.make_async_remote_copy(
                src_ref=stage.at[lo - 1 : hi - 1, peer],
                dst_ref=full.at[lo:hi, dp],
                send_sem=send_b.at[c],
                recv_sem=recv_b.at[c],
                device_id=(peer, mp),
                device_id_type=MESH,
            ).start()
            return carry

        lax.fori_loop(1, N_DP, send_slot, 0)
        if c == 1:
            send_kv_x()
        if c == 2:
            send_kv_y()

    length = lengths[my_sequence]
    scale = 1.0 / math.sqrt(HEAD)
    live = lax.broadcasted_iota(jnp.int32, (CAP, 1), 0) < length

    def halves(t):
        both = full[t].astype(F32)
        return both[:, :ROWS].reshape(CAP, HEAD), both[:, ROWS:].reshape(CAP, HEAD)

    wait_all(recv_kv.at[2], full.at[0, 0 : N_DP - N_Z])
    keys, values = halves(0)
    k_buf[...] = keys.astype(BF16)
    v_buf[...] = values.astype(BF16)
    for c, (lo, hi) in enumerate(CHUNKS):
        wait_all(recv_b.at[c], full.at[lo:hi, 0 : N_DP - 1])
        for t in range(lo, hi):
            j = t - 1
            q_all, g_all = halves(t)
            q_all = q_all.astype(BF16)
            g_all = jnp.where(live, g_all, 0.0).astype(BF16)
            for first in reversed(range(0, CAP, ROW_BLOCK)):
                last = first + ROW_BLOCK
                q, g = q_all[first:last], g_all[first:last]
                k, v = k_buf[:last], v_buf[:last]
                scores = dot_nt(q, k)
                row = lax.broadcasted_iota(jnp.int32, (ROW_BLOCK, last), 0) + first
                col = lax.broadcasted_iota(jnp.int32, (ROW_BLOCK, last), 1)
                scores = jnp.where(col <= row, scores, -1e30)
                top = jnp.max(scores, axis=-1, keepdims=True)
                weights = jnp.exp2((scores - top) * (scale * math.log2(math.e)))
                weights = weights * (1.0 / jnp.sum(weights, axis=-1, keepdims=True))
                probs = weights.astype(BF16)
                out = jnp.where(live[first:last], dot_nn(probs, v), 0.0)
                dprob = dot_nt(g, v)
                delta = jnp.sum(weights * dprob, axis=-1, keepdims=True)
                dscore = (weights * (dprob - delta) * scale).astype(BF16)
                lanes = slice(j * HEAD, (j + 1) * HEAD)
                out_ref[0, first:last, lanes] = out.astype(BF16)
                dq_ref[0, first:last, lanes] = dot_nn(dscore, k).astype(BF16)
                dv_part = dot_tn(probs, g)
                dk_part = dot_tn(dscore, q)
                if j == 0 and last == CAP:
                    dv_acc[...] = dv_part
                    dk_acc[...] = dk_part
                else:
                    dv_acc[:last] += dv_part
                    dk_acc[:last] += dk_part
    dk_ref[0] = dk_acc[...].astype(BF16)
    dv_ref[0] = dv_acc[...].astype(BF16)
    @pl.when(hub)
    def _():
        wait_all(send_kv.at[0], pack_kv.at[0 : PER - 1])
        wait_all(send_kv.at[1], by_z.at[:, 0 : N_MP - 1])

    @pl.when(jnp.logical_not(hub))
    def _():
        wait_all(send_kv.at[0], pack_kv)

    wait_all(send_kv.at[2], full.at[0, 0 : N_DP - N_Z])
    for c, (lo, hi) in enumerate(CHUNKS):
        wait_all(send_a.at[c], held[c].at[:, 0 : SEQS - PER])
        wait_all(send_b.at[c], full.at[lo:hi, 0 : N_DP - 1])


def write_out(*refs):
    sources, results, sem = refs[:4], refs[4:8], refs[8]
    copies = [pltpu.make_async_copy(*pair, sem.at[n]) for n, pair in enumerate(zip(sources, results))]
    for copy in copies:
        copy.start()
    for copy in copies:
        copy.wait()


def shards(q_gen, k_gen, v_gen, grad_gen, lengths, swap_flags):
    vmem = pl.BlockSpec(memory_space=pltpu.VMEM)
    hbm = pl.BlockSpec(memory_space=pl.ANY)
    wide = jax.ShapeDtypeStruct((1, CAP, GROUP * HEAD), BF16)
    narrow = jax.ShapeDtypeStruct((1, CAP, HEAD), BF16)
    chunks = len(CHUNKS)
    results = pl.pallas_call(
        kernel,
        out_shape=tuple(pltpu.VMEM(r.shape, BF16) for r in (wide, wide, narrow, narrow)),
        in_specs=[hbm] * 6,
        out_specs=(vmem, vmem, vmem, vmem),
        scratch_shapes=[
            pltpu.SMEM(swap_flags.shape, jnp.int32),
            pltpu.SMEM(lengths.shape, jnp.int32),
            pltpu.VMEM(q_gen.shape, BF16),
            pltpu.VMEM(k_gen.shape, BF16),
            pltpu.VMEM(v_gen.shape, BF16),
            pltpu.VMEM(grad_gen.shape, BF16),
            pltpu.VMEM((N_MP, GROUP, PER, 2 * ROWS, HEAD), BF16),
            pltpu.VMEM((PER, N_MP, 2 * ROWS, HEAD), BF16),
            pltpu.VMEM((N_Z, N_MP, 2 * ROWS, HEAD), BF16),
            pltpu.VMEM((N_Y, N_Z, 2 * ROWS, HEAD), BF16),
            pltpu.VMEM((N_Y, N_Z, 2 * ROWS, HEAD), BF16),
            pltpu.VMEM((GROUP, N_DP, 2 * ROWS, HEAD), BF16),
            pltpu.VMEM((TILES, N_DP, 2 * ROWS, HEAD), BF16),
            pltpu.VMEM((CAP, HEAD), BF16),
            pltpu.VMEM((CAP, HEAD), BF16),
            pltpu.VMEM((CAP, HEAD), F32),
            pltpu.VMEM((CAP, HEAD), F32),
            pltpu.SemaphoreType.DMA((6,)),
            pltpu.SemaphoreType.DMA((3,)),
            pltpu.SemaphoreType.DMA((3,)),
            pltpu.SemaphoreType.DMA((chunks,)),
            pltpu.SemaphoreType.DMA((chunks,)),
            pltpu.SemaphoreType.DMA((chunks,)),
            pltpu.SemaphoreType.DMA((chunks,)),
            *(pltpu.VMEM((hi - lo, SEQS, 2 * ROWS, HEAD), BF16) for lo, hi in CHUNKS),
        ],
        compiler_params=pltpu.CompilerParams(
            collective_id=0, has_side_effects=True, vmem_limit_bytes=56 * 2**20
        ),
    )(swap_flags, lengths, q_gen, k_gen, v_gen, grad_gen)
    return tuple(
        pl.pallas_call(
            write_out,
            out_shape=(wide, wide, narrow, narrow),
            in_specs=[vmem] * 4,
            out_specs=(hbm, hbm, hbm, hbm),
            scratch_shapes=[
                pltpu.SemaphoreType.DMA((4,)),
            ],
            compiler_params=pltpu.CompilerParams(vmem_limit_bytes=2 * 2**20),
        )(*results)
    )


def solution(mesh):
    rollout = P("mp", "dp", None)
    trainer = P("dp", None, "mp")
    return jax.shard_map(
        shards,
        mesh=mesh,
        in_specs=(rollout, rollout, rollout, rollout, P(), P()),
        out_specs=(trainer, trainer, trainer, trainer),
        check_vma=False,
    )
```

```python
import functools
import math

import jax
import jax.numpy as jnp
from jax import lax
from jax.experimental import pallas as pl
from jax.experimental.pallas import tpu as pltpu
from jax.sharding import PartitionSpec as P

HEAD = 128
N_DP = 64
N_MP = 8
N_Z = 16
N_Y = 4
ROWS = 8
CAP = N_DP * ROWS
SEQS = 64
PER = SEQS // N_MP
GROUP = 4
TILES = 1 + GROUP
CHUNKS = ((1, 2), (2, 3), (3, 4), (4, 5))
ROW_BLOCK = 512
MESH = pl.DeviceIdType.MESH
F32 = jnp.float32
BF16 = jnp.bfloat16


def dot_nt(a, b):
    return lax.dot_general(a, b, (((1,), (1,)), ((), ())), preferred_element_type=F32)


def dot_nn(a, b):
    return lax.dot_general(a, b, (((1,), (0,)), ((), ())), preferred_element_type=F32)


def dot_tn(a, b):
    return lax.dot_general(a, b, (((0,), (0,)), ((), ())), preferred_element_type=F32)


def kernel(
    flags_hbm, lengths_hbm, q_hbm, k_hbm, v_hbm, g_hbm,
    out_ref, dq_ref, dk_ref, dv_ref,
    flags, lengths, q_ref, k_ref, v_ref, g_ref,
    pack, pack_kv, by_z, by_x, by_y, stage, full, k_buf, v_buf, dk_acc, dv_acc,
    load_sem, send_kv, recv_kv, send_a, recv_a, send_b, recv_b, *held,
):
    dp = lax.axis_index("dp")
    mp = lax.axis_index("mp")
    y, z = dp // N_Z, lax.rem(dp, N_Z)
    x, core = mp // 2, lax.rem(mp, 2)
    hub = core == z // PER

    loads = [
        pltpu.make_async_copy(src, dst, load_sem.at[n])
        for n, (src, dst) in enumerate(
            (
                (k_hbm, k_ref), (v_hbm, v_ref), (q_hbm, q_ref), (g_hbm, g_ref),
                (flags_hbm, flags), (lengths_hbm, lengths),
            )
        )
    ]

    def greet_mp(step, carry):
        peer = lax.rem(mp + step, N_MP)
        pl.semaphore_signal(barrier, inc=1, device_id=(dp, peer), device_id_type=MESH)
        return carry

    def greet_dp(step, carry):
        peer = lax.rem(dp + step, N_DP)
        pl.semaphore_signal(barrier, inc=1, device_id=(peer, mp), device_id_type=MESH)
        return carry

    barrier = pltpu.get_barrier_semaphore()
    for load in loads:
        load.start()
    lax.fori_loop(1, N_DP, greet_dp, 0)
    lax.fori_loop(1, N_MP, greet_mp, 0)

    def columns(head):
        return pl.ds(pl.multiple_of(head * HEAD, HEAD), HEAD)

    def join(upper, lower):
        both = jnp.concatenate([upper.astype(F32), lower.astype(F32)], axis=1)
        return both.astype(BF16)

    def fill(t):
        def fill_head(h, carry):
            cols = columns(h * GROUP + t - 1)
            pack[h, t - 1] = join(q_ref[:, :, cols], g_ref[:, :, cols])
            return carry

        lax.fori_loop(0, N_MP, fill_head, 0)

    def fill_kv(h, carry):
        pack_kv[:, h] = join(k_ref[:, :, columns(h)], v_ref[:, :, columns(h)])
        return carry

    def remote(src, dst, send, recv, device):
        pltpu.make_async_remote_copy(
            src_ref=src, dst_ref=dst, send_sem=send, recv_sem=recv, device_id=device, device_id_type=MESH
        ).start()

    def wait_all(sem, ref):
        pltpu.make_async_copy(ref, ref, sem).wait()

    loads[0].wait()
    loads[1].wait()
    lax.fori_loop(0, N_MP, fill_kv, 0)
    pl.semaphore_wait(barrier, N_MP - 1 + N_DP - 1)

    own = lax.rem(z, PER)

    def send_kv_z(step, carry):
        i = lax.rem(own + step, PER)
        remote(pack_kv.at[i], by_z.at[z], send_kv.at[0], recv_kv.at[0], (y * N_Z + core * PER + i, mp))
        return carry

    lax.fori_loop(1, PER, send_kv_z, 0)

    @pl.when(hub)
    def _():
        by_z[z] = pack_kv[own]

    @pl.when(jnp.logical_not(hub))
    def _():
        send_kv_z(0, 0)

    mine = pl.ds(pl.multiple_of(mp * PER, PER), PER)
    for c, (lo, hi) in enumerate(CHUNKS):

        def send_heads(step, carry, c=c, lo=lo, hi=hi):
            peer = lax.rem(mp + step, N_MP)
            pltpu.make_async_remote_copy(
                src_ref=pack.at[peer, lo - 1 : hi - 1],
                dst_ref=held[c].at[:, mine],
                send_sem=send_a.at[c],
                recv_sem=recv_a.at[c],
                device_id=(dp, peer),
                device_id_type=MESH,
            ).start()
            return carry

        if c == 0:
            for load in loads[2:]:
                load.wait()
        for t in range(lo, hi):
            fill(t)
        lax.fori_loop(1, N_MP, send_heads, 0)
        for t in range(lo, hi):
            held[c][t - lo, mine] = pack[mp, t - 1]

    def sequence_of(slot):
        one = jnp.where(flags[1, slot] == 1, slot ^ (N_DP // 4), slot)
        return jnp.where(flags[0, one] == 1, one ^ (N_DP // 2), one)

    def send_kv_x():
        @pl.when(hub)
        def _():
            wait_all(recv_kv.at[0], by_z.at[0 : N_Z - 1])

            def send(step, carry):
                peer = lax.rem(mp + step, N_MP)
                remote(by_z.at[:, peer], by_x.at[x], send_kv.at[1], recv_kv.at[1], (dp, peer))
                return carry

            lax.fori_loop(1, N_MP, send, 0)
            by_x[x] = by_z[:, mp]

    def send_kv_y():
        @pl.when(hub)
        def _():
            wait_all(recv_kv.at[1], by_x.at[0 : N_Y - 1])

        @pl.when(jnp.logical_not(hub))
        def _():
            wait_all(recv_kv.at[1], by_x)

        def send(step, carry):
            to_y = lax.rem(y + step, N_Y)
            slot = to_y * N_Z + z
            by_y[to_y] = by_x[sequence_of(slot) // N_Z]
            remote(by_y.at[to_y], full.at[0, from_here], send_kv.at[2], recv_kv.at[2], (slot, mp))
            return carry

        from_here = pl.ds(pl.multiple_of(y * N_Z, N_Z), N_Z)
        lax.fori_loop(1, N_Y, send, 0)
        full[0, from_here] = by_x[my_sequence // N_Z]

    my_sequence = sequence_of(dp)
    senders = []
    for c, (lo, hi) in enumerate(CHUNKS):

        def send_slot(step, carry, c=c, lo=lo, hi=hi):
            turn, dy = step // N_Y, lax.rem(step, N_Y)
            j = (turn - 1) // 2
            wrapped = jnp.maximum(z - 7, 0)
            up = jnp.where(j < wrapped, j, jnp.where(wrapped == 0, z + 1 + j, N_Z - 1 - (j - wrapped)))
            low = jnp.minimum(z, 7)
            down = jnp.where(j < low, wrapped + j, N_Z - 1 - (j - low))
            to_z = jnp.where(turn == 0, z, jnp.where(lax.rem(turn, 2) == 1, up, down))
            peer = lax.rem(y + dy, N_Y) * N_Z + to_z
            sequence = sequence_of(peer)
            for t in range(lo, hi):
                stage[t - 1, peer] = held[c][t - lo, sequence]
            pltpu.make_async_remote_copy(
                src_ref=stage.at[lo - 1 : hi - 1, peer],
                dst_ref=full.at[lo:hi, dp],
                send_sem=send_b.at[c],
                recv_sem=recv_b.at[c],
                device_id=(peer, mp),
                device_id_type=MESH,
            ).start()
            return carry

        senders.append(send_slot)

    def take(c):
        lo, hi = CHUNKS[c]
        wait_all(recv_a.at[c], held[c].at[:, 0 : SEQS - PER])
        for t in range(lo, hi):
            full[t, dp] = held[c][t - lo, my_sequence]

    take(0)
    lax.fori_loop(1, N_DP, senders[0], 0)
    take(1)
    lax.fori_loop(1, N_DP, senders[1], 0)
    send_kv_x()
    take(2)
    take(3)
    turn_at = jnp.where(z >= N_Z // 2, N_DP // 2, N_DP)
    lax.fori_loop(1, turn_at, senders[2], 0)
    lax.fori_loop(1, turn_at, senders[3], 0)
    send_kv_y()
    lax.fori_loop(turn_at, N_DP, senders[2], 0)
    lax.fori_loop(turn_at, N_DP, senders[3], 0)

    length = lengths[my_sequence]
    scale = 1.0 / math.sqrt(HEAD)
    live = lax.broadcasted_iota(jnp.int32, (CAP, 1), 0) < length

    def halves(t):
        both = full[t].astype(F32)
        return both[:, :ROWS].reshape(CAP, HEAD), both[:, ROWS:].reshape(CAP, HEAD)

    wait_all(recv_kv.at[2], full.at[0, 0 : N_DP - N_Z])
    keys, values = halves(0)
    k_buf[...] = keys.astype(BF16)
    v_buf[...] = values.astype(BF16)
    for c, (lo, hi) in enumerate(CHUNKS):
        wait_all(recv_b.at[c], full.at[lo:hi, 0 : N_DP - 1])
        for t in range(lo, hi):
            j = t - 1
            q_all, g_all = halves(t)
            q_all = q_all.astype(BF16)
            g_all = jnp.where(live, g_all, 0.0).astype(BF16)
            for first in reversed(range(0, CAP, ROW_BLOCK)):
                last = first + ROW_BLOCK
                q, g = q_all[first:last], g_all[first:last]
                k, v = k_buf[:last], v_buf[:last]
                scores = dot_nt(q, k)
                row = lax.broadcasted_iota(jnp.int32, (ROW_BLOCK, last), 0) + first
                col = lax.broadcasted_iota(jnp.int32, (ROW_BLOCK, last), 1)
                scores = jnp.where(col <= row, scores, -1e30)
                top = jnp.max(scores, axis=-1, keepdims=True)
                weights = jnp.exp2((scores - top) * (scale * math.log2(math.e)))
                weights = weights * (1.0 / jnp.sum(weights, axis=-1, keepdims=True))
                probs = weights.astype(BF16)
                out = jnp.where(live[first:last], dot_nn(probs, v), 0.0)
                dprob = dot_nt(g, v)
                delta = jnp.sum(weights * dprob, axis=-1, keepdims=True)
                dscore = (weights * (dprob - delta) * scale).astype(BF16)
                lanes = slice(j * HEAD, (j + 1) * HEAD)
                out_ref[0, first:last, lanes] = out.astype(BF16)
                dq_ref[0, first:last, lanes] = dot_nn(dscore, k).astype(BF16)
                dv_part = dot_tn(probs, g)
                dk_part = dot_tn(dscore, q)
                if j == 0 and last == CAP:
                    dv_acc[...] = dv_part
                    dk_acc[...] = dk_part
                else:
                    dv_acc[:last] += dv_part
                    dk_acc[:last] += dk_part
    dk_ref[0] = dk_acc[...].astype(BF16)
    dv_ref[0] = dv_acc[...].astype(BF16)
    @pl.when(hub)
    def _():
        wait_all(send_kv.at[0], pack_kv.at[0 : PER - 1])
        wait_all(send_kv.at[1], by_z.at[:, 0 : N_MP - 1])

    @pl.when(jnp.logical_not(hub))
    def _():
        wait_all(send_kv.at[0], pack_kv)

    wait_all(send_kv.at[2], full.at[0, 0 : N_DP - N_Z])
    for c, (lo, hi) in enumerate(CHUNKS):
        wait_all(send_a.at[c], held[c].at[:, 0 : SEQS - PER])
        wait_all(send_b.at[c], full.at[lo:hi, 0 : N_DP - 1])


def write_out(*refs):
    sources, results, sem = refs[:4], refs[4:8], refs[8]
    copies = [pltpu.make_async_copy(*pair, sem.at[n]) for n, pair in enumerate(zip(sources, results))]
    for copy in copies:
        copy.start()
    for copy in copies:
        copy.wait()


def shards(q_gen, k_gen, v_gen, grad_gen, lengths, swap_flags):
    vmem = pl.BlockSpec(memory_space=pltpu.VMEM)
    hbm = pl.BlockSpec(memory_space=pl.ANY)
    wide = jax.ShapeDtypeStruct((1, CAP, GROUP * HEAD), BF16)
    narrow = jax.ShapeDtypeStruct((1, CAP, HEAD), BF16)
    chunks = len(CHUNKS)
    results = pl.pallas_call(
        kernel,
        out_shape=tuple(pltpu.VMEM(r.shape, BF16) for r in (wide, wide, narrow, narrow)),
        in_specs=[hbm] * 6,
        out_specs=(vmem, vmem, vmem, vmem),
        scratch_shapes=[
            pltpu.SMEM(swap_flags.shape, jnp.int32),
            pltpu.SMEM(lengths.shape, jnp.int32),
            pltpu.VMEM(q_gen.shape, BF16),
            pltpu.VMEM(k_gen.shape, BF16),
            pltpu.VMEM(v_gen.shape, BF16),
            pltpu.VMEM(grad_gen.shape, BF16),
            pltpu.VMEM((N_MP, GROUP, PER, 2 * ROWS, HEAD), BF16),
            pltpu.VMEM((PER, N_MP, 2 * ROWS, HEAD), BF16),
            pltpu.VMEM((N_Z, N_MP, 2 * ROWS, HEAD), BF16),
            pltpu.VMEM((N_Y, N_Z, 2 * ROWS, HEAD), BF16),
            pltpu.VMEM((N_Y, N_Z, 2 * ROWS, HEAD), BF16),
            pltpu.VMEM((GROUP, N_DP, 2 * ROWS, HEAD), BF16),
            pltpu.VMEM((TILES, N_DP, 2 * ROWS, HEAD), BF16),
            pltpu.VMEM((CAP, HEAD), BF16),
            pltpu.VMEM((CAP, HEAD), BF16),
            pltpu.VMEM((CAP, HEAD), F32),
            pltpu.VMEM((CAP, HEAD), F32),
            pltpu.SemaphoreType.DMA((6,)),
            pltpu.SemaphoreType.DMA((3,)),
            pltpu.SemaphoreType.DMA((3,)),
            pltpu.SemaphoreType.DMA((chunks,)),
            pltpu.SemaphoreType.DMA((chunks,)),
            pltpu.SemaphoreType.DMA((chunks,)),
            pltpu.SemaphoreType.DMA((chunks,)),
            *(pltpu.VMEM((hi - lo, SEQS, 2 * ROWS, HEAD), BF16) for lo, hi in CHUNKS),
        ],
        compiler_params=pltpu.CompilerParams(
            collective_id=0, has_side_effects=True, vmem_limit_bytes=56 * 2**20
        ),
    )(swap_flags, lengths, q_gen, k_gen, v_gen, grad_gen)
    return tuple(
        pl.pallas_call(
            write_out,
            out_shape=(wide, wide, narrow, narrow),
            in_specs=[vmem] * 4,
            out_specs=(hbm, hbm, hbm, hbm),
            scratch_shapes=[
                pltpu.SemaphoreType.DMA((4,)),
            ],
            compiler_params=pltpu.CompilerParams(vmem_limit_bytes=2 * 2**20),
        )(*results)
    )


def solution(mesh):
    rollout = P("mp", "dp", None)
    trainer = P("dp", None, "mp")
    return jax.shard_map(
        shards,
        mesh=mesh,
        in_specs=(rollout, rollout, rollout, rollout, P(), P()),
        out_specs=(trainer, trainer, trainer, trainer),
        check_vma=False,
    )
```

```python
import functools
import math

import jax
import jax.numpy as jnp
from jax import lax
from jax.experimental import pallas as pl
from jax.experimental.pallas import tpu as pltpu
from jax.sharding import PartitionSpec as P

HEAD = 128
N_DP = 64
N_MP = 8
N_Z = 16
N_Y = 4
ROWS = 8
CAP = N_DP * ROWS
SEQS = 64
PER = SEQS // N_MP
GROUP = 4
TILES = 1 + GROUP
CHUNKS = ((1, 2), (2, 3), (3, 4), (4, 5))
ROW_BLOCK = 512
MESH = pl.DeviceIdType.MESH
F32 = jnp.float32
BF16 = jnp.bfloat16


def dot_nt(a, b):
    return lax.dot_general(a, b, (((1,), (1,)), ((), ())), preferred_element_type=F32)


def dot_nn(a, b):
    return lax.dot_general(a, b, (((1,), (0,)), ((), ())), preferred_element_type=F32)


def dot_tn(a, b):
    return lax.dot_general(a, b, (((0,), (0,)), ((), ())), preferred_element_type=F32)


def kernel(
    flags_hbm, lengths_hbm, q_hbm, k_hbm, v_hbm, g_hbm,
    out_ref, dq_ref, dk_ref, dv_ref,
    flags, lengths, q_ref, k_ref, v_ref, g_ref,
    pack, pack_kv, by_z, by_x, by_y, stage, full, k_buf, v_buf, dk_acc, dv_acc,
    load_sem, send_kv, recv_kv, send_a, recv_a, send_b, recv_b, *held,
):
    dp = lax.axis_index("dp")
    mp = lax.axis_index("mp")
    y, z = dp // N_Z, lax.rem(dp, N_Z)
    x, core = mp // 2, lax.rem(mp, 2)
    hub = core == z // PER

    loads = [
        pltpu.make_async_copy(src, dst, load_sem.at[n])
        for n, (src, dst) in enumerate(
            (
                (k_hbm, k_ref), (v_hbm, v_ref), (q_hbm, q_ref), (g_hbm, g_ref),
                (flags_hbm, flags), (lengths_hbm, lengths),
            )
        )
    ]

    def greet_mp(step, carry):
        peer = lax.rem(mp + step, N_MP)
        pl.semaphore_signal(barrier, inc=1, device_id=(dp, peer), device_id_type=MESH)
        return carry

    def greet_dp(step, carry):
        peer = lax.rem(dp + step, N_DP)
        pl.semaphore_signal(barrier, inc=1, device_id=(peer, mp), device_id_type=MESH)
        return carry

    barrier = pltpu.get_barrier_semaphore()
    for load in loads:
        load.start()
    lax.fori_loop(1, N_DP, greet_dp, 0, unroll=True)
    lax.fori_loop(1, N_MP, greet_mp, 0, unroll=True)

    def columns(head):
        return pl.ds(pl.multiple_of(head * HEAD, HEAD), HEAD)

    def join(upper, lower):
        both = jnp.concatenate([upper.astype(F32), lower.astype(F32)], axis=1)
        return both.astype(BF16)

    def fill(t):
        def fill_head(h, carry):
            cols = columns(h * GROUP + t - 1)
            pack[h, t - 1] = join(q_ref[:, :, cols], g_ref[:, :, cols])
            return carry

        lax.fori_loop(0, N_MP, fill_head, 0)

    def fill_kv(h, carry):
        pack_kv[:, h] = join(k_ref[:, :, columns(h)], v_ref[:, :, columns(h)])
        return carry

    def remote(src, dst, send, recv, device):
        pltpu.make_async_remote_copy(
            src_ref=src, dst_ref=dst, send_sem=send, recv_sem=recv, device_id=device, device_id_type=MESH
        ).start()

    def wait_all(sem, ref):
        pltpu.make_async_copy(ref, ref, sem).wait()

    loads[0].wait()
    loads[1].wait()
    lax.fori_loop(0, N_MP, fill_kv, 0)
    pl.semaphore_wait(barrier, N_MP - 1 + N_DP - 1)

    own = lax.rem(z, PER)

    def send_kv_z(step, carry):
        i = lax.rem(own + step, PER)
        remote(pack_kv.at[i], by_z.at[z], send_kv.at[0], recv_kv.at[0], (y * N_Z + core * PER + i, mp))
        return carry

    lax.fori_loop(1, PER, send_kv_z, 0)

    @pl.when(hub)
    def _():
        by_z[z] = pack_kv[own]

    @pl.when(jnp.logical_not(hub))
    def _():
        send_kv_z(0, 0)

    mine = pl.ds(pl.multiple_of(mp * PER, PER), PER)
    for c, (lo, hi) in enumerate(CHUNKS):

        def send_heads(step, carry, c=c, lo=lo, hi=hi):
            peer = lax.rem(mp + step, N_MP)
            pltpu.make_async_remote_copy(
                src_ref=pack.at[peer, lo - 1 : hi - 1],
                dst_ref=held[c].at[:, mine],
                send_sem=send_a.at[c],
                recv_sem=recv_a.at[c],
                device_id=(dp, peer),
                device_id_type=MESH,
            ).start()
            return carry

        if c == 0:
            for load in loads[2:]:
                load.wait()
        for t in range(lo, hi):
            fill(t)
        lax.fori_loop(1, N_MP, send_heads, 0)
        for t in range(lo, hi):
            held[c][t - lo, mine] = pack[mp, t - 1]

    def sequence_of(slot):
        one = jnp.where(flags[1, slot] == 1, slot ^ (N_DP // 4), slot)
        return jnp.where(flags[0, one] == 1, one ^ (N_DP // 2), one)

    def send_kv_x():
        @pl.when(hub)
        def _():
            wait_all(recv_kv.at[0], by_z.at[0 : N_Z - 1])

            def send(step, carry):
                peer = lax.rem(mp + step, N_MP)
                remote(by_z.at[:, peer], by_x.at[x], send_kv.at[1], recv_kv.at[1], (dp, peer))
                return carry

            lax.fori_loop(1, N_MP, send, 0)
            by_x[x] = by_z[:, mp]

    def send_kv_y():
        @pl.when(hub)
        def _():
            wait_all(recv_kv.at[1], by_x.at[0 : N_Y - 1])

        @pl.when(jnp.logical_not(hub))
        def _():
            wait_all(recv_kv.at[1], by_x)

        def send(step, carry):
            to_y = lax.rem(y + step, N_Y)
            slot = to_y * N_Z + z
            by_y[to_y] = by_x[sequence_of(slot) // N_Z]
            remote(by_y.at[to_y], full.at[0, from_here], send_kv.at[2], recv_kv.at[2], (slot, mp))
            return carry

        from_here = pl.ds(pl.multiple_of(y * N_Z, N_Z), N_Z)
        lax.fori_loop(1, N_Y, send, 0)
        full[0, from_here] = by_x[my_sequence // N_Z]

    my_sequence = sequence_of(dp)
    senders = []
    for c, (lo, hi) in enumerate(CHUNKS):

        def send_slot(step, carry, c=c, lo=lo, hi=hi):
            turn, dy = step // N_Y, lax.rem(step, N_Y)
            j = (turn - 1) // 2
            wrapped = jnp.maximum(z - 7, 0)
            up = jnp.where(j < wrapped, j, jnp.where(wrapped == 0, z + 1 + j, N_Z - 1 - (j - wrapped)))
            low = jnp.minimum(z, 7)
            down = jnp.where(j < low, wrapped + j, N_Z - 1 - (j - low))
            to_z = jnp.where(turn == 0, z, jnp.where(lax.rem(turn, 2) == 1, up, down))
            peer = lax.rem(y + dy, N_Y) * N_Z + to_z
            sequence = sequence_of(peer)
            for t in range(lo, hi):
                stage[t - 1, peer] = held[c][t - lo, sequence]
            pltpu.make_async_remote_copy(
                src_ref=stage.at[lo - 1 : hi - 1, peer],
                dst_ref=full.at[lo:hi, dp],
                send_sem=send_b.at[c],
                recv_sem=recv_b.at[c],
                device_id=(peer, mp),
                device_id_type=MESH,
            ).start()
            return carry

        senders.append(send_slot)

    def take(c):
        lo, hi = CHUNKS[c]
        wait_all(recv_a.at[c], held[c].at[:, 0 : SEQS - PER])
        for t in range(lo, hi):
            full[t, dp] = held[c][t - lo, my_sequence]

    take(0)
    lax.fori_loop(1, N_DP, senders[0], 0)
    take(1)
    lax.fori_loop(1, N_DP, senders[1], 0)
    send_kv_x()
    take(2)
    take(3)
    turn_at = jnp.where((z >= N_Z // 2) | (core == 0), N_DP // 2, N_DP)
    lax.fori_loop(1, turn_at, senders[2], 0)
    lax.fori_loop(1, turn_at, senders[3], 0)
    send_kv_y()
    lax.fori_loop(turn_at, N_DP, senders[2], 0)
    lax.fori_loop(turn_at, N_DP, senders[3], 0)

    length = lengths[my_sequence]
    scale = 1.0 / math.sqrt(HEAD)
    live = lax.broadcasted_iota(jnp.int32, (CAP, 1), 0) < length

    def halves(t):
        both = full[t].astype(F32)
        return both[:, :ROWS].reshape(CAP, HEAD), both[:, ROWS:].reshape(CAP, HEAD)

    wait_all(recv_kv.at[2], full.at[0, 0 : N_DP - N_Z])
    keys, values = halves(0)
    k_buf[...] = keys.astype(BF16)
    v_buf[...] = values.astype(BF16)
    for c, (lo, hi) in enumerate(CHUNKS):
        wait_all(recv_b.at[c], full.at[lo:hi, 0 : N_DP - 1])
        for t in range(lo, hi):
            j = t - 1
            q_all, g_all = halves(t)
            q_all = q_all.astype(BF16)
            g_all = jnp.where(live, g_all, 0.0).astype(BF16)
            for first in reversed(range(0, CAP, ROW_BLOCK)):
                last = first + ROW_BLOCK
                q, g = q_all[first:last], g_all[first:last]
                k, v = k_buf[:last], v_buf[:last]
                scores = dot_nt(q, k)
                row = lax.broadcasted_iota(jnp.int32, (ROW_BLOCK, last), 0) + first
                col = lax.broadcasted_iota(jnp.int32, (ROW_BLOCK, last), 1)
                scores = jnp.where(col <= row, scores, -1e30)
                top = jnp.max(scores, axis=-1, keepdims=True)
                weights = jnp.exp2((scores - top) * (scale * math.log2(math.e)))
                weights = weights * (1.0 / jnp.sum(weights, axis=-1, keepdims=True))
                probs = weights.astype(BF16)
                out = jnp.where(live[first:last], dot_nn(probs, v), 0.0)
                dprob = dot_nt(g, v)
                delta = jnp.sum(weights * dprob, axis=-1, keepdims=True)
                dscore = (weights * (dprob - delta) * scale).astype(BF16)
                lanes = slice(j * HEAD, (j + 1) * HEAD)
                out_ref[0, first:last, lanes] = out.astype(BF16)
                dq_ref[0, first:last, lanes] = dot_nn(dscore, k).astype(BF16)
                dv_part = dot_tn(probs, g)
                dk_part = dot_tn(dscore, q)
                if j == 0 and last == CAP:
                    dv_acc[...] = dv_part
                    dk_acc[...] = dk_part
                else:
                    dv_acc[:last] += dv_part
                    dk_acc[:last] += dk_part
    dk_ref[0] = dk_acc[...].astype(BF16)
    dv_ref[0] = dv_acc[...].astype(BF16)
    @pl.when(hub)
    def _():
        wait_all(send_kv.at[0], pack_kv.at[0 : PER - 1])
        wait_all(send_kv.at[1], by_z.at[:, 0 : N_MP - 1])

    @pl.when(jnp.logical_not(hub))
    def _():
        wait_all(send_kv.at[0], pack_kv)

    wait_all(send_kv.at[2], full.at[0, 0 : N_DP - N_Z])
    for c, (lo, hi) in enumerate(CHUNKS):
        wait_all(send_a.at[c], held[c].at[:, 0 : SEQS - PER])
        wait_all(send_b.at[c], full.at[lo:hi, 0 : N_DP - 1])


def write_out(*refs):
    sources, results, sem = refs[:4], refs[4:8], refs[8]
    copies = [pltpu.make_async_copy(*pair, sem.at[n]) for n, pair in enumerate(zip(sources, results))]
    for copy in copies:
        copy.start()
    for copy in copies:
        copy.wait()


def shards(q_gen, k_gen, v_gen, grad_gen, lengths, swap_flags):
    vmem = pl.BlockSpec(memory_space=pltpu.VMEM)
    hbm = pl.BlockSpec(memory_space=pl.ANY)
    wide = jax.ShapeDtypeStruct((1, CAP, GROUP * HEAD), BF16)
    narrow = jax.ShapeDtypeStruct((1, CAP, HEAD), BF16)
    chunks = len(CHUNKS)
    results = pl.pallas_call(
        kernel,
        out_shape=tuple(pltpu.VMEM(r.shape, BF16) for r in (wide, wide, narrow, narrow)),
        in_specs=[hbm] * 6,
        out_specs=(vmem, vmem, vmem, vmem),
        scratch_shapes=[
            pltpu.SMEM(swap_flags.shape, jnp.int32),
            pltpu.SMEM(lengths.shape, jnp.int32),
            pltpu.VMEM(q_gen.shape, BF16),
            pltpu.VMEM(k_gen.shape, BF16),
            pltpu.VMEM(v_gen.shape, BF16),
            pltpu.VMEM(grad_gen.shape, BF16),
            pltpu.VMEM((N_MP, GROUP, PER, 2 * ROWS, HEAD), BF16),
            pltpu.VMEM((PER, N_MP, 2 * ROWS, HEAD), BF16),
            pltpu.VMEM((N_Z, N_MP, 2 * ROWS, HEAD), BF16),
            pltpu.VMEM((N_Y, N_Z, 2 * ROWS, HEAD), BF16),
            pltpu.VMEM((N_Y, N_Z, 2 * ROWS, HEAD), BF16),
            pltpu.VMEM((GROUP, N_DP, 2 * ROWS, HEAD), BF16),
            pltpu.VMEM((TILES, N_DP, 2 * ROWS, HEAD), BF16),
            pltpu.VMEM((CAP, HEAD), BF16),
            pltpu.VMEM((CAP, HEAD), BF16),
            pltpu.VMEM((CAP, HEAD), F32),
            pltpu.VMEM((CAP, HEAD), F32),
            pltpu.SemaphoreType.DMA((6,)),
            pltpu.SemaphoreType.DMA((3,)),
            pltpu.SemaphoreType.DMA((3,)),
            pltpu.SemaphoreType.DMA((chunks,)),
            pltpu.SemaphoreType.DMA((chunks,)),
            pltpu.SemaphoreType.DMA((chunks,)),
            pltpu.SemaphoreType.DMA((chunks,)),
            *(pltpu.VMEM((hi - lo, SEQS, 2 * ROWS, HEAD), BF16) for lo, hi in CHUNKS),
        ],
        compiler_params=pltpu.CompilerParams(
            collective_id=0, has_side_effects=True, vmem_limit_bytes=56 * 2**20
        ),
    )(swap_flags, lengths, q_gen, k_gen, v_gen, grad_gen)
    return tuple(
        pl.pallas_call(
            write_out,
            out_shape=(wide, wide, narrow, narrow),
            in_specs=[vmem] * 4,
            out_specs=(hbm, hbm, hbm, hbm),
            scratch_shapes=[
                pltpu.SemaphoreType.DMA((4,)),
            ],
            compiler_params=pltpu.CompilerParams(vmem_limit_bytes=2 * 2**20),
        )(*results)
    )


def solution(mesh):
    rollout = P("mp", "dp", None)
    trainer = P("dp", None, "mp")
    return jax.shard_map(
        shards,
        mesh=mesh,
        in_specs=(rollout, rollout, rollout, rollout, P(), P()),
        out_specs=(trainer, trainer, trainer, trainer),
        check_vma=False,
    )
```
